32 devices in a mesh: grp: 2 (over y), lat: 4 (over x, core), wid: 4 (over z).
Axes of the slice: x: 2, y: 2, z: 4, core: 2. Of those that a mesh axis runs over, the one named last changes fastest.
Arguments:
- resid: bfloat16 [2048, 8192], P('grp', 'wid'), parts along dimension 0, may hold values from -6 to 6
- weight: bfloat16 [65536, 8192], P(('grp', 'lat'), 'wid'), parts along dimension 0, may hold values from -0.0625 to 0.0625
- enc_bias: float32 [65536], P(('grp', 'lat')), parts along dimension 0, may hold values from -3 to 3
- dec_bias: float32 [8192], P('wid'), may hold values from -3 to 3
- block_ids: int32 [8, 64], P('grp'), parts along dimension 0, may hold values from 0 to 255, as said below
- block_counts: int32 [8], P('grp'), parts along dimension 0, may hold values from 48 to 64, as said below
Outputs:
- grad_weight: bfloat16 [65536, 8192], P(('grp', 'lat'), 'wid'), parts along dimension 0
- grad_bias: float32 [65536], P(('grp', 'lat')), parts along dimension 0
The draws below stay inside these ranges and needn't reach their ends.
There are 2 independent parts, one for each index of `grp`. The reference program is written for one: setup_inputs(seed, part) draws one part's arguments, and reference() takes and returns one part's arrays. A program takes and returns all parts, laid end to end along the dimension named above; an argument that names none is the same for every part. Nothing has to cross between parts.
Inputs may be any that keep to these rules, and one draw needn't show every extreme that they name: `block_ids`: each tile lists 64 distinct blocks in any order, exactly 16 of them in each run of 64 blocks starting at a multiple of 64. `block_counts`: some tile has all 64 entries active.
All inputs are finite; a program needn't handle non-finite values.
Results may differ from the reference program's by a relative error of at most 0.015.
Values may be sent and summed in bfloat16 or wider, within the bound.
A program may use at most 384 MiB of HBM per device.

```python
import jax
import jax.numpy as jnp
from jax import lax

D = 8192
LAT = 32768
BLK = 128
TILE = 256
TILES = 4
MAXB = 64
TOKENS = 1024
N_LAT = 4
N_WID = 4


def draw_block_ids(key, part):
    key = jax.random.fold_in(key, 11)
    per_shard = LAT // BLK // N_LAT
    per_run = MAXB // N_LAT

    def one_tile(tile_key):
        pick_key, order_key = jax.random.split(tile_key)
        picks = jax.vmap(lambda inner: jax.random.permutation(inner, per_shard)[:per_run])(jax.random.split(pick_key, N_LAT))
        listed = (jnp.arange(N_LAT, dtype=jnp.int32)[:, None] * per_shard + picks).reshape(MAXB)
        return jax.random.permutation(order_key, listed)
    listed = jax.vmap(one_tile)(jax.random.split(key, TILES))
    return listed.astype(jnp.int32)


def draw_block_counts(key, part):
    key = jax.random.fold_in(key, 12)
    first_key, second_key = jax.random.split(key)
    drawn = jax.random.randint(first_key, (TILES,), 3 * MAXB // 4, MAXB + 1)
    chosen = jax.random.randint(second_key, (), 0, TILES)
    full = jnp.where(jnp.arange(TILES) == chosen, MAXB, drawn)
    return full.astype(jnp.int32)


def shard_levels(key, shape, cuts, smallest, high):
    def one(position, blocks):
        steps = jax.random.uniform(jax.random.fold_in(jax.random.fold_in(key, 6), position), (blocks,), jnp.float32, smallest / len(cuts), high / len(cuts))
        return jnp.repeat(jnp.exp(steps), shape[position] // blocks).reshape((-1,) + (1,) * (len(shape) - position - 1))

    gain = one(*cuts[0])
    for cut in cuts[1:]:
        gain = gain * one(*cut)
    return gain


def scatter_about(stream_key, shape, deviation, bound, pieces=(), kind=jnp.bfloat16):
    values = deviation * jax.random.normal(stream_key, shape, jnp.float32)
    if pieces:
        values = values * shard_levels(stream_key, shape, pieces, -0.22, 0.18)
    return jnp.clip(values, -bound, bound).astype(kind)


def setup_inputs(seed: int = 0, part: int = 0) -> dict:
    key_of = jax.random.split(jax.random.key(seed), 7)
    part_keys = jax.random.split(jax.random.fold_in(key_of[6], part), 7)
    return {
        "resid": scatter_about(part_keys[0], (TOKENS, D), 1.0, 6.0, ((1, 4),)),
        "weight": scatter_about(part_keys[1], (LAT, D), D ** -0.5, 0.0625, ((0, 4), (1, 4))),
        "enc_bias": scatter_about(part_keys[2], (LAT,), 0.5, 3.0, ((0, 4),), jnp.float32),
        "dec_bias": scatter_about(key_of[3], (D,), 0.5, 3.0, ((0, 4),), jnp.float32),
        "block_ids": draw_block_ids(jax.random.fold_in(jax.random.fold_in(key_of[6], part), 71), part),
        "block_counts": draw_block_counts(jax.random.fold_in(jax.random.fold_in(key_of[6], part), 71), part),
    }


grad_scale = 0.0625


def rounded(value):
    return lax.optimization_barrier(value.astype(jnp.bfloat16)).astype(jnp.float32)


def reference(resid, weight, enc_bias, dec_bias, block_ids, block_counts):
    width_dev = D // N_WID
    per_shard = LAT // BLK // N_LAT
    exact = lax.Precision.HIGHEST
    centred = (resid.astype(jnp.float32) - dec_bias).astype(jnp.bfloat16)
    blocks = weight.reshape(LAT // BLK, BLK, D)
    bias_blocks = enc_bias.reshape(LAT // BLK, BLK)

    def one_tile(tile):
        listed = block_ids[tile]
        valid = (jnp.arange(MAXB, dtype=jnp.int32) < block_counts[tile]).astype(jnp.float32)
        w_slots = blocks[listed].astype(jnp.float32)
        w_split = w_slots.reshape(MAXB, BLK, N_WID, width_dev)
        start = (tile * TILE).astype(jnp.int32)
        x_tile = lax.dynamic_slice_in_dim(centred, start, TILE, 0).astype(jnp.float32)
        raw_tile = lax.dynamic_slice_in_dim(resid, start, TILE, 0).astype(jnp.float32)
        partial_value = jnp.einsum('tkd,sbkd->kstb', x_tile.reshape(TILE, N_WID, width_dev), w_split, precision=exact)
        summed = jnp.sum(rounded(partial_value), axis=0)
        codes = (jnp.maximum(summed + bias_blocks[listed][:, None, :], 0.0) * valid[:, None, None]).astype(jnp.bfloat16)
        code_f = codes.astype(jnp.float32)
        owner = ((listed // per_shard)[:, None] == jnp.arange(N_LAT, dtype=jnp.int32)[None, :]).astype(jnp.float32)
        parts = jnp.einsum('sr,stb,sbd->rtd', owner, code_f, w_slots, precision=exact)
        recon = jnp.sum(rounded(parts), axis=0) + dec_bias
        error = (recon - raw_tile).astype(jnp.bfloat16)
        error_f = error.astype(jnp.float32)
        slope_parts = jnp.einsum('tkd,sbkd->kstb', error_f.reshape(TILE, N_WID, width_dev), w_split, precision=exact)
        slope = jnp.sum(rounded(slope_parts), axis=0)
        d_codes = jnp.where(codes > 0, slope, 0.0).astype(jnp.bfloat16)
        d_f = d_codes.astype(jnp.float32)
        terms = jnp.einsum('stb,td->sbd', code_f, error_f, precision=exact) + jnp.einsum('stb,td->sbd', d_f, x_tile, precision=exact)
        return terms, jnp.sum(d_f, axis=1)

    terms, bias_terms = lax.map(one_tile, jnp.arange(TILES, dtype=jnp.int32))
    flat = block_ids.reshape(-1)
    grad = jnp.zeros((LAT // BLK, BLK, D), jnp.float32).at[flat].add(terms.reshape(TILES * MAXB, BLK, D))
    grad_b = jnp.zeros((LAT // BLK, BLK), jnp.float32).at[flat].add(bias_terms.reshape(TILES * MAXB, BLK))
    grad_weight = (grad * grad_scale).reshape(LAT, D).astype(jnp.bfloat16)
    grad_bias = (grad_b * grad_scale).reshape(LAT)
    return grad_weight, grad_bias
```

```python
import functools

import jax
import jax.numpy as jnp
from jax import lax
from jax.experimental import pallas as pl
from jax.experimental.pallas import tpu as pltpu
from jax.sharding import PartitionSpec as P

BLK = 128
TILE = 256
MAXB = 64
VMEM = 50 * 1024 * 1024

grad_scale = 0.0625
f32 = jnp.float32
bf16 = jnp.bfloat16
ANY = pl.BlockSpec(memory_space=pl.ANY)


def fetch(ids, w_ref, buf, sem, slots, first=0):
    copies = []
    for s in range(slots):
        start = pl.multiple_of(ids[first + s] * BLK, BLK)
        copies.append(
            pltpu.make_async_copy(
                w_ref.at[pl.ds(start, BLK), :], buf.at[pl.ds(s * BLK, BLK), :], sem.at[s]
            )
        )
    for copy in copies:
        copy.start()
    return copies


def to_slots_kernel(slots, group, first, ids, x_ref, w_ref, *refs):
    out_ref, buf, sem = refs[-3:]
    copies = fetch(ids, w_ref, buf, sem, slots, first)
    for g in range(0, slots, group):
        for copy in copies[g : g + group]:
            copy.wait()
        rows = pl.ds(g * BLK, group * BLK)
        out_ref[rows, :] = lax.dot_general(
            buf[rows, :], x_ref[...], (((1,), (1,)), ((), ())), preferred_element_type=f32
        ).astype(bf16)


def to_slots(ids, x, weight, first, slots, after=()):
    width = weight.shape[1]
    return pl.pallas_call(
        functools.partial(to_slots_kernel, slots, min(4, slots), first),
        out_shape=jax.ShapeDtypeStruct((slots * BLK, TILE), bf16),
        in_specs=[
            pl.BlockSpec(memory_space=pltpu.SMEM),
            pl.BlockSpec(memory_space=pltpu.VMEM),
            ANY,
        ]
        + [ANY] * len(after),
        out_specs=pl.BlockSpec(memory_space=pltpu.VMEM),
        scratch_shapes=[
            pltpu.VMEM((slots * BLK, width), bf16),
            pltpu.SemaphoreType.DMA((slots,)),
        ],
        compiler_params=pltpu.CompilerParams(vmem_limit_bytes=VMEM),
        cost_estimate=pl.CostEstimate(
            flops=2 * slots * BLK * TILE * width,
            bytes_accessed=2 * (slots * BLK * (width + TILE) + TILE * width),
            transcendentals=0,
        ),
    )(ids, x, weight, *after)


def to_width_kernel(slots, group, ids, codes_ref, w_ref, *refs):
    out_ref, buf, acc, sem = refs[-4:]
    copies = fetch(ids, w_ref, buf, sem, slots)
    for g in range(0, slots, group):
        for copy in copies[g : g + group]:
            copy.wait()
        rows = pl.ds(g * BLK, group * BLK)
        part = lax.dot_general(
            codes_ref[rows, :], buf[rows, :], (((0,), (0,)), ((), ())), preferred_element_type=f32
        )
        if g == 0:
            acc[...] = part
        else:
            acc[...] += part
    out_ref[...] = acc[...].astype(bf16)


def to_width(ids, codes, weight, after=()):
    width = weight.shape[1]
    slots = codes.shape[0] // BLK
    return pl.pallas_call(
        functools.partial(to_width_kernel, slots, min(4, slots)),
        out_shape=jax.ShapeDtypeStruct((TILE, width), bf16),
        in_specs=[
            pl.BlockSpec(memory_space=pltpu.SMEM),
            pl.BlockSpec(memory_space=pltpu.VMEM),
            ANY,
        ]
        + [ANY] * len(after),
        out_specs=pl.BlockSpec(memory_space=pltpu.VMEM),
        scratch_shapes=[
            pltpu.VMEM((slots * BLK, width), bf16),
            pltpu.VMEM((TILE, width), f32),
            pltpu.SemaphoreType.DMA((slots,)),
        ],
        compiler_params=pltpu.CompilerParams(vmem_limit_bytes=VMEM),
        cost_estimate=pl.CostEstimate(
            flops=2 * slots * BLK * TILE * width,
            bytes_accessed=2 * (slots * BLK * (width + TILE) + TILE * width),
            transcendentals=0,
        ),
    )(ids, codes, weight, *after)


def add_grads_kernel(slots, n_terms, ids, valid, g_in, *refs):
    g_ref, mark, buf, in_sem, out_sem = refs[-5:]
    mark[...] = jnp.zeros_like(mark)

    def window(s):
        return pl.ds(pl.multiple_of(ids[s] * BLK, BLK), BLK)

    def slot_rows(s):
        return pl.ds(s * BLK, BLK)

    for s in range(slots):

        @pl.when(valid[s] > 0)
        def _(s=s):
            pltpu.make_async_copy(
                g_ref.at[window(s), :], buf.at[slot_rows(s), :], in_sem.at[s]
            ).start()

    for s in range(slots):

        @pl.when(valid[s] > 0)
        def _(s=s):
            rows = slot_rows(s)
            part = jnp.dot(refs[0][rows, :], refs[1][...], preferred_element_type=f32)
            for k in range(1, n_terms):
                part += jnp.dot(
                    refs[2 * k][rows, :], refs[2 * k + 1][...], preferred_element_type=f32
                )
            pltpu.make_async_copy(g_ref.at[window(s), :], buf.at[rows, :], in_sem.at[s]).wait()
            buf[rows, :] = (buf[rows, :].astype(f32) + part * grad_scale).astype(bf16)
            pltpu.make_async_copy(buf.at[rows, :], g_ref.at[window(s), :], out_sem.at[s]).start()

    for s in range(slots):

        @pl.when(valid[s] > 0)
        def _(s=s):
            pltpu.make_async_copy(
                buf.at[slot_rows(s), :], g_ref.at[window(s), :], out_sem.at[s]
            ).wait()


def add_grads(ids, valid, terms, grad, after=()):
    width = grad.shape[1]
    operands = [a for pair in terms for a in pair]
    slots = operands[0].shape[0] // BLK
    return pl.pallas_call(
        functools.partial(add_grads_kernel, slots, len(terms)),
        out_shape=[
            jax.ShapeDtypeStruct(grad.shape, bf16),
            jax.ShapeDtypeStruct((8, BLK), f32),
        ],
        in_specs=[
            pl.BlockSpec(memory_space=pltpu.SMEM),
            pl.BlockSpec(memory_space=pltpu.SMEM),
            ANY,
        ]
        + [pl.BlockSpec(memory_space=pltpu.VMEM)] * len(operands)
        + [ANY] * len(after),
        out_specs=[ANY, pl.BlockSpec(memory_space=pltpu.VMEM)],
        scratch_shapes=[
            pltpu.VMEM((slots * BLK, width), bf16),
            pltpu.SemaphoreType.DMA((slots,)),
            pltpu.SemaphoreType.DMA((slots,)),
        ],
        input_output_aliases={2: 0},
        compiler_params=pltpu.CompilerParams(vmem_limit_bytes=VMEM),
        cost_estimate=pl.CostEstimate(
            flops=2 * len(terms) * slots * BLK * TILE * width,
            bytes_accessed=4 * slots * BLK * width,
            transcendentals=0,
        ),
    )(ids, valid, grad, *operands, *after)


def sum_wid(part, finish):
    if lax.axis_size("wid") != 4:
        total = finish(lax.psum(part, "wid").astype(f32))
        return total, total, total
    me = lax.axis_index("wid")
    inner = (me == 1) | (me == 2)
    outer_part = lax.ppermute(part, "wid", [(0, 1), (3, 2)])
    pair = (part.astype(f32) + outer_part.astype(f32)).astype(bf16)
    other = lax.ppermute(pair, "wid", [(1, 2), (2, 1)])
    result = finish(pair.astype(f32) + other.astype(f32))
    back = lax.ppermute(result, "wid", [(1, 0), (2, 3)])
    return pair, result, jnp.where(inner, result, back)


def sum_lat(part, raw, dec_bias):
    n = lax.axis_size("lat")
    if n != 4:
        total = lax.psum(part, "lat").astype(f32)
        error = (total + dec_bias - raw.astype(f32)).astype(bf16)
        return error, error
    core = lax.rem(lax.axis_index("lat"), 2)
    cores = [(0, 1), (1, 0), (2, 3), (3, 2)]
    chips = [(0, 2), (2, 0), (1, 3), (3, 1)]
    first = core == 0
    top, bottom = jnp.split(part, 2, axis=0)
    raw_top, raw_bottom = jnp.split(raw, 2, axis=0)
    mine, theirs = jnp.where(first, top, bottom), jnp.where(first, bottom, top)
    mine = (mine.astype(f32) + lax.ppermute(theirs, "lat", cores).astype(f32)).astype(bf16)
    total = mine.astype(f32) + lax.ppermute(mine, "lat", chips).astype(f32)
    error = (total + dec_bias - jnp.where(first, raw_top, raw_bottom).astype(f32)).astype(bf16)
    error_other = lax.ppermute(error, "lat", cores)
    return mine, jnp.concatenate(
        [jnp.where(first, error, error_other), jnp.where(first, error_other, error)], axis=0
    )


def local(resid, weight, enc_bias, dec_bias, block_ids, block_counts):
    tiles = block_ids.shape[0]
    width = resid.shape[1]
    per_shard = weight.shape[0] // BLK
    slots = MAXB // lax.axis_size("lat")
    local_ids = block_ids - lax.axis_index("lat") * per_shard
    slot_iota = jnp.arange(MAXB, dtype=jnp.int32)
    in_shard = (
        (local_ids >= 0) & (local_ids < per_shard) & (slot_iota[None, :] < block_counts[:, None])
    )
    before = slot_iota[None, :] < slot_iota[:, None]
    place = jnp.sum((in_shard[:, None, :] & before[None]).astype(jnp.int32), axis=2)
    select = (place[:, None, :] == jnp.arange(slots, dtype=jnp.int32)[None, :, None]) & in_shard[
        :, None, :
    ]
    slot_block = jnp.sum(jnp.where(select, local_ids[:, None, :], 0), axis=2)
    slot_valid = jnp.any(select, axis=2)
    valid_i = slot_valid.astype(jnp.int32)
    table = (
        (slot_block[:, :, None] == jnp.arange(per_shard, dtype=jnp.int32)) & slot_valid[:, :, None]
    )
    bias_blocks = enc_bias.reshape(per_shard, BLK)
    bias_slots = bias_blocks[slot_block]

    halves = 1
    sub = slots // halves
    raw = [resid[n * TILE : (n + 1) * TILE] for n in range(tiles)]
    centred = [(r.astype(f32) - dec_bias).astype(bf16) for r in raw]
    chunks = [(n, h) for n in range(tiles) for h in range(halves)]
    count = len(chunks)
    parts, pairs, results, final = [], [], [], []
    codes, error, d_codes = [], [], []
    after_chunk = {}

    def put(position, value):
        after_chunk.setdefault(position, []).append(value)

    def step(x, n, h, finish):
        c = len(parts)
        after = list(after_chunk.get(c, []))
        for stage, lag in ((pairs, 2), (results, 3), (final, 4)):
            if c >= lag:
                after.append(stage[c - lag])
        part = to_slots(slot_block[n], x, weight, h * sub, sub, after)
        parts.append(part)
        pair, result, done = sum_wid(part, finish)
        pairs.append(pair)
        results.append(result)
        final.append(done)

    def decode(n):
        codes.append(jnp.concatenate(final[n * halves : (n + 1) * halves], axis=0))
        recon = to_width(slot_block[n], codes[n], weight, [parts[-1]])
        mine, err = sum_lat(recon, raw[n], dec_bias)
        error.append(err)
        put(count + halves * n - 2, recon)
        put(count + halves * n - 1, mine)

    for n, h in chunks:
        own = slice(h * sub, (h + 1) * sub)
        bias = bias_slots[n, own].reshape(sub * BLK, 1)
        keep = jnp.repeat(slot_valid[n, own], BLK).reshape(sub * BLK, 1)

        def finish(total, bias=bias, keep=keep):
            return jnp.where(keep, jnp.maximum(total + bias, 0.0), 0.0).astype(bf16)

        step(centred[n], n, h, finish)
        if halves == 2 and len(parts) == count - 2:
            decode(0)
    decode(len(codes))
    grad_now = [jnp.zeros((per_shard * BLK, width), bf16)]

    def add(n, with_codes, with_d, after):
        terms = [(codes[n], error[n])] * with_codes + [(d_codes[n], centred[n])] * with_d
        grad_now[0], mark = add_grads(slot_block[n], valid_i[n], terms, grad_now[0], after)
        put(len(parts), mark)

    for n, h in chunks:
        active = codes[n][h * sub * BLK : (h + 1) * sub * BLK] > 0

        def finish(total, active=active):
            return jnp.where(active, total, 0.0).astype(bf16)

        step(error[n], n, h, finish)
        if h == halves - 1:
            if len(codes) < tiles:
                decode(len(codes))
            lo = count + n * halves
            d_codes.append(jnp.concatenate(final[lo : lo + halves], axis=0))
        if halves == 2 and len(parts) == 2 * count - 2:
            add(0, True, True, [parts[-1]])

    last = tiles - 1
    for n in range(1 if halves == 2 else 0, last):
        if n == last - 1:
            add(last, True, False, [parts[-1], pairs[-1]])
        add(n, True, True, [parts[-1]] if n < last - 1 else [results[-1]])
    add(last, False, True, [])
    grad = grad_now[0]
    bias_terms = jnp.stack(
        [jnp.sum(d.astype(f32).reshape(slots, BLK, TILE), axis=2) for d in d_codes]
    ).reshape(tiles * slots, BLK)
    grad_b = jnp.dot(
        table.reshape(tiles * slots, per_shard).astype(f32).T,
        bias_terms,
        precision=lax.Precision.HIGHEST,
        preferred_element_type=f32,
    )
    return (grad, (grad_b * grad_scale).reshape(per_shard * BLK))


def solution(mesh):
    in_specs = (
        P("grp", "wid"),
        P(("grp", "lat"), "wid"),
        P(("grp", "lat")),
        P("wid"),
        P("grp", None),
        P("grp"),
    )
    out_specs = (P(("grp", "lat"), "wid"), P(("grp", "lat")))
    return jax.shard_map(local, mesh=mesh, in_specs=in_specs, out_specs=out_specs, check_vma=False)
```
